128 devices in a mesh: dp: 8 (over z, y_lo), tensor: 16 (over x, y_hi, core).
Axes of the slice: x: 4, y: 4 (y_hi: 2, y_lo: 2; y = y_hi * 2 + y_lo), z: 4, core: 2. Of those that a mesh axis runs over, the one named last changes fastest.
Arguments:
- tokens: bfloat16 [1024, 8192], P('tensor', 'dp'), may hold values from -6 to 6
- out_grad: bfloat16 [1024, 8192], P('tensor', 'dp'), may hold values from -6 to 6
- gate_pre: bfloat16 [1024, 29568], P('dp', 'tensor'), may hold values from -6 to 6
- up_pre: bfloat16 [1024, 29568], P('dp', 'tensor'), may hold values from -6 to 6
- gate_weight: bfloat16 [8192, 29568], P('dp', 'tensor'), may hold values from -0.0625 to 0.0625
- up_weight: bfloat16 [8192, 29568], P('dp', 'tensor'), may hold values from -0.0625 to 0.0625
- down_weight: bfloat16 [29568, 8192], P('tensor', 'dp'), may hold values from -0.03125 to 0.03125
Outputs:
- in_grad: bfloat16 [1024, 8192], P('tensor', 'dp')
- gate_wgrad: bfloat16 [8192, 29568], P('dp', 'tensor')
- up_wgrad: bfloat16 [8192, 29568], P('dp', 'tensor')
- down_wgrad: bfloat16 [29568, 8192], P('tensor', 'dp')
The draws below stay inside these ranges and needn't reach their ends.
All inputs are finite; a program needn't handle non-finite values.
Results may differ from the reference program's by a relative error of at most 0.0049.
Values may be sent and summed in bfloat16 or wider, within the bound.
No kernel may reach another device: no remote copies, remote signals or barrier semaphores. Data moves between devices by JAX's collectives and lax.ppermute only.
A program may use at most 128 MiB of HBM per device.

```python
import jax
import jax.numpy as jnp

D = 8192
FF = 29568
TOKENS = 1024


def with_spikes(drawn, own_key, source, target, shards_of, factor):
    def block_of(position):
        return (jnp.arange(drawn.shape[position]) // (drawn.shape[position] // shards_of)).reshape((-1,) + (1,) * (drawn.ndim - 1 - position))

    one_side = jax.random.permutation(own_key, shards_of)[block_of(target)]
    far = (block_of(target) + shards_of // 2) % shards_of
    return jnp.where((block_of(source) == one_side) | (block_of(source) == far), factor * drawn, drawn)


def block_scale(own_key, shape, shards, smallest, top_value):
    def one(dim, shards_of):
        heights = jax.random.uniform(jax.random.fold_in(jax.random.fold_in(own_key, 6), dim), (shards_of,), jnp.float32, smallest / len(shards), top_value / len(shards))
        return jnp.repeat(jnp.exp(heights), shape[dim] // shards_of).reshape((-1,) + (1,) * (len(shape) - dim - 1))

    loudness = one(*shards[0])
    for cut in shards[1:]:
        loudness = loudness * one(*cut)
    return loudness


def centred(own_key, dims, spread, reach, split=(), dtype=jnp.bfloat16):
    result = jax.random.normal(own_key, dims, jnp.float32) * spread
    if len(split) > 0:
        result = block_scale(own_key, dims, split, -0.22, 0.18) * result
    return jnp.clip(result, min=-reach, max=reach).astype(dtype)


def heavy_noise(stream_key, shape, width, most, cuts, heavy, dtype=jnp.bfloat16):
    array = width * jax.random.normal(stream_key, shape, jnp.float32)
    if cuts:
        array = array * block_scale(stream_key, shape, cuts, -0.22, 0.18)
    return jnp.clip(with_spikes(array, jax.random.fold_in(stream_key, 3), *heavy), -most, most).astype(dtype)


def setup_inputs(seed: int = 0) -> dict:
    splits = jax.random.split(jax.random.key(seed), 8)
    return {
        "tokens": centred(splits[0], (TOKENS, D), 1.0, 6.0, ((0, 16), (1, 8))),
        "out_grad": heavy_noise(splits[1], (TOKENS, D), 1.0, 6.0, ((0, 16), (1, 8)), (1, 0, 16, 2.0)),
        "gate_pre": heavy_noise(splits[2], (TOKENS, FF), 1.5, 6.0, ((0, 8), (1, 16)), (1, 0, 16, 2.0)),
        "up_pre": centred(splits[3], (TOKENS, FF), 1.0, 6.0, ((0, 8), (1, 16))),
        "gate_weight": centred(splits[4], (D, FF), D ** -0.5, 0.0625, ((0, 8), (1, 16))),
        "up_weight": centred(splits[5], (D, FF), D ** -0.5, 0.0625, ((0, 8), (1, 16))),
        "down_weight": centred(splits[6], (FF, D), FF ** -0.5, 0.03125, ((0, 16), (1, 8))),
    }


def reference(tokens, out_grad, gate_pre, up_pre, gate_weight, up_weight, down_weight):
    factor = 1.0 / jnp.sqrt(jnp.float32(TOKENS))
    hidden_grad = jnp.dot(out_grad, down_weight.T, preferred_element_type=jnp.float32)
    gate = gate_pre.astype(jnp.float32)
    upper = up_pre.astype(jnp.float32)
    sigma = jax.nn.sigmoid(gate)
    gate_grad = (hidden_grad * upper * sigma * (1.0 + gate * (1.0 - sigma))).astype(jnp.bfloat16)
    up_grad = (hidden_grad * gate * sigma).astype(jnp.bfloat16)
    hidden = (gate * sigma * upper).astype(jnp.bfloat16)
    in_grad = jnp.dot(gate_grad, gate_weight.T, preferred_element_type=jnp.float32)
    in_grad = in_grad + jnp.dot(up_grad, up_weight.T, preferred_element_type=jnp.float32)
    gate_wgrad = jnp.dot(tokens.T, gate_grad, preferred_element_type=jnp.float32) * factor
    up_wgrad = jnp.dot(tokens.T, up_grad, preferred_element_type=jnp.float32) * factor
    down_wgrad = jnp.dot(hidden.T, out_grad, preferred_element_type=jnp.float32) * factor
    return (in_grad.astype(jnp.bfloat16), gate_wgrad.astype(jnp.bfloat16), up_wgrad.astype(jnp.bfloat16), down_wgrad.astype(jnp.bfloat16))
```

```python
import jax
import jax.numpy as jnp
from jax import lax
from jax.sharding import PartitionSpec as P


R1A, R1B, R2A = 512, 512, 416


def dp_move(value, dz, dy):
    pairs = [(i, ((i // 2 + dz) % 4) * 2 + ((i % 2) ^ dy)) for i in range(8)]
    return lax.ppermute(value, "dp", pairs)


def tensor_move(value, dx, dh, dc):
    pairs = [(i, ((i // 4 + dx) % 4) * 4 + (((i // 2) % 2) ^ dh) * 2 + ((i % 2) ^ dc)) for i in range(16)]
    return lax.ppermute(value, "tensor", pairs)


def cat(*values):
    return jnp.concatenate(values, axis=-2)


def split_rows(value):
    a, b, c = R1A, R1A + R1B, R1A + R1B + R2A
    return value[..., :a, :], value[..., a:b, :], value[..., b:c, :], value[..., c:, :]


def gather_dp(own):
    r1 = R1A + R1B
    full = own.shape[-2]
    y0 = dp_move(own, 0, 1)
    zp = dp_move(own, 1, 0)
    zm = dp_move(own, -1, 0)
    pa, pb, pc, pd = split_rows(zp)
    ma, mb, mc, md = split_rows(zm)
    first = y0[..., :r1, :]
    sp = dp_move(cat(first, pa, pc), 1, 0)
    sm = dp_move(cat(first, mb, md), -1, 0)
    sy = dp_move(cat(pc, pd, mc, md), 0, 1)
    n2 = full - r1
    p1 = sp[..., :r1, :]
    m1 = sm[..., :r1, :]
    two_a, two_c = sp[..., r1 : r1 + R1A, :], sp[..., r1 + R1A :, :]
    two_b, two_d = sm[..., r1 : r1 + R1B, :], sm[..., r1 + R1B :, :]
    tp = dp_move(p1[..., :R1A, :], 1, 0)
    tm = dp_move(m1[..., R1A:, :], -1, 0)
    ty = dp_move(cat(two_c, two_d), 0, 1)
    return [
        own,
        y0,
        zm,
        cat(m1, sy[..., n2:, :]),
        cat(two_a, two_b, two_c, two_d),
        cat(tp, tm, ty),
        zp,
        cat(p1, sy[..., :n2, :]),
    ]


def reduce_dp(parts):
    bf, f32 = jnp.bfloat16, jnp.float32
    q = [list(split_rows(p)) for p in parts]
    own, y0, zp, zpy, z2, z2y, zm, zmy = q
    tp = dp_move(z2y[0].astype(bf), 1, 0)
    tm = dp_move(z2y[1].astype(bf), -1, 0)
    ty = dp_move(cat(z2y[2], z2y[3]).astype(bf), 0, 1)
    zpy[0] = zpy[0] + tp.astype(f32)
    zmy[1] = zmy[1] + tm.astype(f32)
    n = R2A
    z2[2] = z2[2] + ty[:n].astype(f32)
    z2[3] = z2[3] + ty[n:].astype(f32)
    r1, r2 = R1A + R1B, parts[0].shape[0] - R1A - R1B
    sy = dp_move(cat(zmy[2], zmy[3], zpy[2], zpy[3]).astype(bf), 0, 1)
    sp = dp_move(cat(zpy[0], zpy[1], z2[0], z2[2]).astype(bf), 1, 0)
    sm = dp_move(cat(zmy[0], zmy[1], z2[1], z2[3]).astype(bf), -1, 0)
    spf, smf, syf = sp.astype(f32), sm.astype(f32), sy.astype(f32)
    y0[0] = y0[0] + spf[:R1A] + smf[:R1A]
    y0[1] = y0[1] + spf[R1A:r1] + smf[R1A:r1]
    zp[0] = zp[0] + spf[r1 : r1 + R1A]
    zp[2] = zp[2] + spf[r1 + R1A :] + syf[r2 : r2 + n]
    zp[3] = zp[3] + syf[r2 + n :]
    zm[1] = zm[1] + smf[r1 : r1 + R1B]
    zm[2] = zm[2] + syf[:n]
    zm[3] = zm[3] + smf[r1 + R1B :] + syf[n:r2]
    up = dp_move(cat(*zp).astype(bf), 1, 0)
    um = dp_move(cat(*zm).astype(bf), -1, 0)
    uy = dp_move(cat(*y0).astype(bf), 0, 1)
    return parts[0] + up.astype(f32) + um.astype(f32) + uy.astype(f32)


def gather_tensor(own):
    h0 = tensor_move(own, 0, 1, 0)
    xp = tensor_move(own, 1, 0, 0)
    xm = tensor_move(own, -1, 0, 0)
    sp = tensor_move(cat(h0, xp[:32]), 1, 0, 0)
    sm = tensor_move(cat(h0, xm[32:]), -1, 0, 0)
    tp = tensor_move(sp[:32], 1, 0, 0)
    tm = tensor_move(sm[32:64], -1, 0, 0)
    mine = jnp.stack(
        [own, h0, xm, sm[:64], cat(sp[64:], sm[64:]), cat(tp, tm), xp, sp[:64]]
    ).reshape(4, 2, 64, own.shape[1])
    other = tensor_move(mine, 0, 0, 1)
    core = lax.rem(lax.axis_index("tensor"), 2)
    return jnp.where(
        core == 0, jnp.concatenate([mine, other], axis=2), jnp.concatenate([other, mine], axis=2)
    )


def reduce_tensor(terms):
    bf, f32 = jnp.bfloat16, jnp.float32
    core = lax.rem(lax.axis_index("tensor"), 2)
    low, high = terms[:, :, :64], terms[:, :, 64:]
    mine = jnp.where(core == 0, low, high)
    theirs = jnp.where(core == 0, high, low)
    s = mine + tensor_move(theirs.astype(bf), 0, 0, 1).astype(f32)
    tp = tensor_move(s[2, :, :32].astype(bf), 1, 0, 0)
    tm = tensor_move(s[2, :, 32:].astype(bf), -1, 0, 0)
    one = jnp.concatenate([s[1, :, :32] + tp.astype(f32), s[1, :, 32:]], axis=1)
    three = jnp.concatenate([s[3, :, :32], s[3, :, 32:] + tm.astype(f32)], axis=1)
    up = tensor_move(one.astype(bf), 1, 0, 0)
    um = tensor_move(three.astype(bf), -1, 0, 0)
    local = s[0] + up.astype(f32) + um.astype(f32)
    return local[0] + tensor_move(local[1].astype(bf), 0, 1, 0).astype(f32)


def turn(blocks, shift, flip):
    rolled = lax.dynamic_slice_in_dim(jnp.concatenate([blocks, blocks], axis=0), shift, 4, axis=0)
    return jnp.where(flip == 0, rolled, rolled[:, ::-1])


def per_device(tokens, out_grad, gate_pre, up_pre, gate_weight, up_weight, down_weight):
    f32, bf = jnp.float32, jnp.bfloat16
    d, t = lax.axis_index("dp"), lax.axis_index("tensor")
    z, lo, x, hi = d // 2, d % 2, t // 4, (t // 2) % 2
    width = tokens.shape[1]
    count = 1024
    factor = 1.0 / jnp.sqrt(f32(count))
    pre = gather_dp(jnp.stack([gate_pre.T, up_pre.T]))
    grads = turn(gather_tensor(out_grad), (z - x) % 4, lo ^ hi).reshape(count, width)
    all_tokens = lax.all_gather(tokens, "tensor", axis=0, tiled=True).reshape(4, 2, 128, width)
    all_tokens = turn(all_tokens, z, lo).reshape(count, width)
    terms = lax.dot_general(down_weight, grads, (((1,), (1,)), ((), ())), preferred_element_type=f32)
    own = reduce_dp([terms[:, i * 128 : (i + 1) * 128] for i in range(8)])
    hidden_grad = jnp.concatenate(gather_dp(own.astype(bf)), axis=-1).astype(f32)
    pre = jnp.concatenate(pre, axis=-1)
    gate, upper = pre[0].astype(f32), pre[1].astype(f32)
    sigma = jax.nn.sigmoid(gate)
    gate_grad = (hidden_grad * upper * sigma * (1.0 + gate * (1.0 - sigma))).astype(bf)
    up_grad = (hidden_grad * gate * sigma).astype(bf)
    hidden = (gate * sigma * upper).astype(bf)

    def wgrad(left, right):
        out = lax.dot_general(left, right, (((1,), (0,)), ((), ())), preferred_element_type=f32)
        return (out * factor).astype(bf)

    def back(left, right):
        return lax.dot_general(left, right, (((0,), (0,)), ((), ())), preferred_element_type=f32)

    down_wgrad = wgrad(hidden, grads)
    partial = back(gate_grad, gate_weight.T) + back(up_grad, up_weight.T)
    partial = turn(partial.reshape(4, 2, 128, width), (x - z) % 4, lo ^ hi)
    in_grad = reduce_tensor(partial).astype(bf)
    gate_wgrad = wgrad(gate_grad, all_tokens).T
    up_wgrad = wgrad(up_grad, all_tokens).T
    return (in_grad, gate_wgrad, up_wgrad, down_wgrad)


def solution(mesh):
    placed = (
        P("tensor", "dp"),
        P("tensor", "dp"),
        P("dp", "tensor"),
        P("dp", "tensor"),
        P("dp", "tensor"),
        P("dp", "tensor"),
        P("tensor", "dp"),
    )
    return jax.shard_map(
        per_device,
        mesh=mesh,
        in_specs=placed,
        out_specs=(P("tensor", "dp"), P("dp", "tensor"), P("dp", "tensor"), P("tensor", "dp")),
        check_vma=False,
    )
```

```python
import jax
import jax.numpy as jnp
from jax import lax
from jax.sharding import PartitionSpec as P


R1A, R1B, R2A = 512, 512, 416


def dp_move(value, dz, dy):
    pairs = [(i, ((i // 2 + dz) % 4) * 2 + ((i % 2) ^ dy)) for i in range(8)]
    return lax.ppermute(value, "dp", pairs)


def tensor_move(value, dx, dh, dc):
    pairs = [(i, ((i // 4 + dx) % 4) * 4 + (((i // 2) % 2) ^ dh) * 2 + ((i % 2) ^ dc)) for i in range(16)]
    return lax.ppermute(value, "tensor", pairs)


def cat(*values):
    return jnp.concatenate(values, axis=-2)


def split_rows(value):
    a, b, c = R1A, R1A + R1B, R1A + R1B + R2A
    return value[..., :a, :], value[..., a:b, :], value[..., b:c, :], value[..., c:, :]


def gather_dp(own, before_third):
    r1 = R1A + R1B
    full = own.shape[-2]
    y0 = dp_move(own, 0, 1)
    zp = dp_move(own, 1, 0)
    zm = dp_move(own, -1, 0)
    pa, pb, pc, pd = split_rows(zp)
    ma, mb, mc, md = split_rows(zm)
    first = y0[..., :r1, :]
    sp = dp_move(cat(first, pa, pc), 1, 0)
    sm = dp_move(cat(first, mb, md), -1, 0)
    sy = dp_move(cat(pc, pd, mc, md), 0, 1)
    sp, sm, sy = after((sp, sm, sy), before_third)
    n2 = full - r1
    p1 = sp[..., :r1, :]
    m1 = sm[..., :r1, :]
    two_a, two_c = sp[..., r1 : r1 + R1A, :], sp[..., r1 + R1A :, :]
    two_b, two_d = sm[..., r1 : r1 + R1B, :], sm[..., r1 + R1B :, :]
    tp = dp_move(p1[..., :R1A, :], 1, 0)
    tm = dp_move(m1[..., R1A:, :], -1, 0)
    ty = dp_move(cat(two_c, two_d), 0, 1)
    return [
        own,
        y0,
        zm,
        cat(m1, sy[..., n2:, :]),
        cat(two_a, two_b, two_c, two_d),
        cat(tp, tm, ty),
        zp,
        cat(p1, sy[..., :n2, :]),
    ]


def first_sums(parts):
    far = [p.astype(jnp.bfloat16) for p in split_rows(parts[5])]
    return dp_move(far[0], 1, 0), dp_move(far[1], -1, 0), dp_move(cat(far[2], far[3]), 0, 1)


def reduce_dp(parts, first):
    bf, f32 = jnp.bfloat16, jnp.float32
    q = [list(split_rows(p)) for p in parts]
    own, y0, zp, zpy, z2, z2y, zm, zmy = q
    tp, tm, ty = first
    zpy[0] = zpy[0] + tp.astype(f32)
    zmy[1] = zmy[1] + tm.astype(f32)
    n = R2A
    z2[2] = z2[2] + ty[:n].astype(f32)
    z2[3] = z2[3] + ty[n:].astype(f32)
    r1, r2 = R1A + R1B, parts[0].shape[0] - R1A - R1B
    sy = dp_move(cat(zmy[2], zmy[3], zpy[2], zpy[3]).astype(bf), 0, 1)
    sp = dp_move(cat(zpy[0], zpy[1], z2[0], z2[2]).astype(bf), 1, 0)
    sm = dp_move(cat(zmy[0], zmy[1], z2[1], z2[3]).astype(bf), -1, 0)
    spf, smf, syf = sp.astype(f32), sm.astype(f32), sy.astype(f32)
    y0[0] = y0[0] + spf[:R1A] + smf[:R1A]
    y0[1] = y0[1] + spf[R1A:r1] + smf[R1A:r1]
    zp[0] = zp[0] + spf[r1 : r1 + R1A]
    zp[2] = zp[2] + spf[r1 + R1A :] + syf[r2 : r2 + n]
    zp[3] = zp[3] + syf[r2 + n :]
    zm[1] = zm[1] + smf[r1 : r1 + R1B]
    zm[2] = zm[2] + syf[:n]
    zm[3] = zm[3] + smf[r1 + R1B :] + syf[n:r2]
    up = dp_move(cat(*zp).astype(bf), 1, 0)
    um = dp_move(cat(*zm).astype(bf), -1, 0)
    uy = dp_move(cat(*y0).astype(bf), 0, 1)
    return parts[0] + up.astype(f32) + um.astype(f32) + uy.astype(f32)


def ring_gather(own):
    full, half = own.shape[0], 928
    y0 = dp_move(own, 0, 1)
    zp = dp_move(own, 1, 0)
    zm = dp_move(own, -1, 0)
    sp = dp_move(cat(y0, zp[:half]), 1, 0)
    sm = dp_move(cat(y0, zm[half:]), -1, 0)
    low, high = dp_move(sp[:half], 1, 0), dp_move(sm[half:full], -1, 0)
    return [own, y0, zm, sm[:full], cat(sp[full:], sm[full:]), cat(low, high), zp, sp[:full]]


def sum_chips(blocks):
    same_core = [[chip * 2 + k for chip in range(8)] for k in range(2)]
    moved = lax.all_to_all(blocks.astype(jnp.bfloat16), "tensor", 0, 0, axis_index_groups=same_core)
    return moved.astype(jnp.float32).sum(0)


ORDER = ((0, 1, 2, 6), (3, 7, 4), (5,))


def after(value, *first):
    return lax.optimization_barrier((value, *first))[0]


def gather_tensor(own, core):
    h0 = tensor_move(own, 0, 1, 0)
    xp = tensor_move(own, 1, 0, 0)
    xm = tensor_move(own, -1, 0, 0)
    sp = tensor_move(cat(h0, xp[:, :32]), 1, 0, 0)
    sm = tensor_move(cat(h0, xm[:, 32:]), -1, 0, 0)
    tp = tensor_move(sp[:, :32], 1, 0, 0)
    tm = tensor_move(sm[:, 32:64], -1, 0, 0)
    parts = [own, h0, xm, sm[:, :64], cat(sp[:, 64:], sm[:, 64:]), cat(tp, tm), xp, sp[:, :64]]
    mine = jnp.stack(parts, axis=1)
    other = tensor_move(mine, 0, 0, 1)
    low, high = jnp.where(core == 0, mine, other), jnp.where(core == 0, other, mine)
    shape = (4, 2, 128, own.shape[-1])
    return [jnp.concatenate([low[i], high[i]], axis=1).reshape(shape) for i in range(2)]


def turn(blocks, shift, flip):
    rolled = lax.dynamic_slice_in_dim(jnp.concatenate([blocks, blocks], axis=0), shift & 3, 4, axis=0)
    return jnp.where(flip == 0, rolled, rolled[:, ::-1])


def per_device(tokens, out_grad, gate_pre, up_pre, gate_weight, up_weight, down_weight):
    f32, bf = jnp.float32, jnp.bfloat16
    d, t = lax.axis_index("dp"), lax.axis_index("tensor")
    z, lo, x, hi, core = d >> 1, d & 1, t >> 2, (t >> 1) & 1, t & 1
    width = tokens.shape[1]
    count = 1024
    factor = 1.0 / jnp.sqrt(f32(count))
    grads, all_tokens = gather_tensor(jnp.stack([out_grad, tokens]), core)
    grads = turn(grads, z - x, lo ^ hi).reshape(count, width)
    all_tokens = turn(all_tokens, z - x, lo ^ hi)
    terms = lax.dot_general(down_weight, grads, (((1,), (1,)), ((), ())), preferred_element_type=f32)
    terms = [terms[:, i * 128 : (i + 1) * 128] for i in range(8)]
    first = first_sums(terms)
    pre = gather_dp(jnp.stack([gate_pre.T, up_pre.T]), first)
    own = reduce_dp(terms, first)

    def wgrad(left, right):
        out = lax.dot_general(left, right, (((1,), (0,)), ((), ())), preferred_element_type=f32)
        return (out * factor).astype(bf)

    def back(left, right):
        return lax.dot_general(left, right, (((0,), (0,)), ((), ())), preferred_element_type=f32)

    gate, upper = (jnp.concatenate([p[i] for p in pre], axis=-1) for i in range(2))
    gate, upper = lax.optimization_barrier((gate, upper))
    gate, upper = gate.astype(f32), upper.astype(f32)
    hidden = (gate * jax.nn.sigmoid(gate) * upper).astype(bf)
    down_wgrad = wgrad(hidden, grads)
    sums = ring_gather(own.astype(bf))
    partials, gate_grads, up_grads = [], [], []
    for keys in ORDER:
        gate32 = jnp.concatenate([pre[k][0] for k in keys], axis=-1).astype(f32)
        upper32 = jnp.concatenate([pre[k][1] for k in keys], axis=-1).astype(f32)
        hidden_grad = jnp.concatenate([sums[k] for k in keys], axis=-1)
        if keys == ORDER[1]:
            hidden_grad = after(hidden_grad, down_wgrad)
        hidden_grad = hidden_grad.astype(f32)
        sigma = jax.nn.sigmoid(gate32)
        gate_grad = (hidden_grad * upper32 * sigma * (1.0 + gate32 * (1.0 - sigma))).astype(bf)
        up_grad = (hidden_grad * gate32 * sigma).astype(bf)
        partial = back(gate_grad, gate_weight.T) + back(up_grad, up_weight.T)
        partials += [partial[i * 128 : (i + 1) * 128] for i in range(len(keys))]
        gate_grads.append(gate_grad)
        up_grads.append(up_grad)
    keys = sum(ORDER, ())
    partial = jnp.stack([partials[keys.index(k)] for k in range(8)])
    theirs = lax.dynamic_slice_in_dim(partial, 64 * (1 - core), 64, axis=1)
    mine = lax.dynamic_slice_in_dim(partial, 64 * core, 64, axis=1)
    total = mine + tensor_move(theirs, 0, 0, 1)
    in_grad = sum_chips(turn(total.reshape(4, 2, 64, width), -z, lo).reshape(8, 64, width)).astype(bf)
    held = jnp.concatenate([all_tokens[k // 2, k % 2] for k in keys])
    gate_grads, up_grads = after(gate_grads, total), after(up_grads, total)
    gate_wgrad = wgrad(jnp.concatenate(gate_grads, axis=1), held).T
    up_wgrad = wgrad(jnp.concatenate(up_grads, axis=1), held).T
    return (in_grad, gate_wgrad, up_wgrad, down_wgrad)


def solution(mesh):
    placed = (
        P("tensor", "dp"),
        P("tensor", "dp"),
        P("dp", "tensor"),
        P("dp", "tensor"),
        P("dp", "tensor"),
        P("dp", "tensor"),
        P("tensor", "dp"),
    )
    return jax.shard_map(
        per_device,
        mesh=mesh,
        in_specs=placed,
        out_specs=(P("tensor", "dp"), P("dp", "tensor"), P("dp", "tensor"), P("tensor", "dp")),
        check_vma=False,
    )
```

```python
import jax
import jax.numpy as jnp
from jax import lax
from jax.sharding import PartitionSpec as P


R1A, R1B, R2A = 512, 512, 416


def dp_move(value, dz, dy):
    pairs = [(i, ((i // 2 + dz) % 4) * 2 + ((i % 2) ^ dy)) for i in range(8)]
    return lax.ppermute(value, "dp", pairs)


def tensor_move(value, dx, dh, dc):
    pairs = [(i, ((i // 4 + dx) % 4) * 4 + (((i // 2) % 2) ^ dh) * 2 + ((i % 2) ^ dc)) for i in range(16)]
    return lax.ppermute(value, "tensor", pairs)


def cat(*values):
    return jnp.concatenate(values, axis=-2)


def split_rows(value):
    a, b, c = R1A, R1A + R1B, R1A + R1B + R2A
    return value[..., :a, :], value[..., a:b, :], value[..., b:c, :], value[..., c:, :]


def gather_dp(own, before_third):
    r1 = R1A + R1B
    full = own.shape[-2]
    y0 = dp_move(own, 0, 1)
    zp = dp_move(own, 1, 0)
    zm = dp_move(own, -1, 0)
    pa, pb, pc, pd = split_rows(zp)
    ma, mb, mc, md = split_rows(zm)
    first = y0[..., :r1, :]
    sp = dp_move(cat(first, pa, pc), 1, 0)
    sm = dp_move(cat(first, mb, md), -1, 0)
    sy = dp_move(cat(pc, pd, mc, md), 0, 1)
    sp, sm, sy = after((sp, sm, sy), before_third)
    n2 = full - r1
    p1 = sp[..., :r1, :]
    m1 = sm[..., :r1, :]
    two_a, two_c = sp[..., r1 : r1 + R1A, :], sp[..., r1 + R1A :, :]
    two_b, two_d = sm[..., r1 : r1 + R1B, :], sm[..., r1 + R1B :, :]
    tp = dp_move(p1[..., :R1A, :], 1, 0)
    tm = dp_move(m1[..., R1A:, :], -1, 0)
    ty = dp_move(cat(two_c, two_d), 0, 1)
    return [
        own,
        y0,
        zm,
        cat(m1, sy[..., n2:, :]),
        cat(two_a, two_b, two_c, two_d),
        cat(tp, tm, ty),
        zp,
        cat(p1, sy[..., :n2, :]),
    ]


def first_sums(parts):
    far = [p.astype(jnp.bfloat16) for p in split_rows(parts[5])]
    return dp_move(far[0], 1, 0), dp_move(far[1], -1, 0), dp_move(cat(far[2], far[3]), 0, 1)


def reduce_dp(parts, first):
    bf, f32 = jnp.bfloat16, jnp.float32
    q = [list(split_rows(p)) for p in parts]
    own, y0, zp, zpy, z2, z2y, zm, zmy = q
    tp, tm, ty = first
    zpy[0] = zpy[0] + tp.astype(f32)
    zmy[1] = zmy[1] + tm.astype(f32)
    n = R2A
    z2[2] = z2[2] + ty[:n].astype(f32)
    z2[3] = z2[3] + ty[n:].astype(f32)
    r1, r2 = R1A + R1B, parts[0].shape[0] - R1A - R1B
    sy = dp_move(cat(zmy[2], zmy[3], zpy[2], zpy[3]).astype(bf), 0, 1)
    sp = dp_move(cat(zpy[0], zpy[1], z2[0], z2[2]).astype(bf), 1, 0)
    sm = dp_move(cat(zmy[0], zmy[1], z2[1], z2[3]).astype(bf), -1, 0)
    spf, smf, syf = sp.astype(f32), sm.astype(f32), sy.astype(f32)
    y0[0] = y0[0] + spf[:R1A] + smf[:R1A]
    y0[1] = y0[1] + spf[R1A:r1] + smf[R1A:r1]
    zp[0] = zp[0] + spf[r1 : r1 + R1A]
    zp[2] = zp[2] + spf[r1 + R1A :] + syf[r2 : r2 + n]
    zp[3] = zp[3] + syf[r2 + n :]
    zm[1] = zm[1] + smf[r1 : r1 + R1B]
    zm[2] = zm[2] + syf[:n]
    zm[3] = zm[3] + smf[r1 + R1B :] + syf[n:r2]
    up = dp_move(cat(*zp).astype(bf), 1, 0)
    um = dp_move(cat(*zm).astype(bf), -1, 0)
    uy = dp_move(cat(*y0).astype(bf), 0, 1)
    return parts[0] + up.astype(f32) + um.astype(f32) + uy.astype(f32)


def ring_gather(own):
    full, half = own.shape[0], 928
    y0 = dp_move(own, 0, 1)
    zp = dp_move(own, 1, 0)
    zm = dp_move(own, -1, 0)
    sp = dp_move(cat(y0, zp[:half]), 1, 0)
    sm = dp_move(cat(y0, zm[half:]), -1, 0)
    low, high = dp_move(sp[:half], 1, 0), dp_move(sm[half:full], -1, 0)
    return [own, y0, zm, sm[:full], cat(sp[full:], sm[full:]), cat(low, high), zp, sp[:full]]


def sum_chips(blocks):
    same_core = [[chip * 2 + k for chip in range(8)] for k in range(2)]
    moved = lax.all_to_all(blocks.astype(jnp.bfloat16), "tensor", 0, 0, axis_index_groups=same_core)
    return moved.astype(jnp.float32).sum(0)


ORDER = ((0, 1, 2, 6), (3, 7, 4), (5,))


def after(value, *first):
    return lax.optimization_barrier((value, *first))[0]


def gather_tensor(own, core):
    h0 = tensor_move(own, 0, 1, 0)
    pair = cat(own, h0)
    xp = tensor_move(pair, 1, 0, 0)
    xm = tensor_move(pair, -1, 0, 0)
    tp = tensor_move(cat(xp[:, :32], xp[:, 64:96]), 1, 0, 0)
    tm = tensor_move(cat(xm[:, 32:64], xm[:, 96:]), -1, 0, 0)
    far = cat(tp[:, :32], tm[:, :32], tp[:, 32:], tm[:, 32:])
    parts = [part[:, 64 * h : 64 * h + 64] for part in (pair, xm, far, xp) for h in range(2)]
    mine = jnp.stack(parts, axis=1)
    other = tensor_move(mine, 0, 0, 1)
    low, high = jnp.where(core == 0, mine, other), jnp.where(core == 0, other, mine)
    shape = (4, 2, 128, own.shape[-1])
    return [jnp.concatenate([low[i], high[i]], axis=1).reshape(shape) for i in range(2)]


def turn(blocks, shift, flip):
    rolled = lax.dynamic_slice_in_dim(jnp.concatenate([blocks, blocks], axis=0), shift & 3, 4, axis=0)
    return jnp.where(flip == 0, rolled, rolled[:, ::-1])


def per_device(tokens, out_grad, gate_pre, up_pre, gate_weight, up_weight, down_weight):
    f32, bf = jnp.float32, jnp.bfloat16
    d, t = lax.axis_index("dp"), lax.axis_index("tensor")
    z, lo, x, hi, core = d >> 1, d & 1, t >> 2, (t >> 1) & 1, t & 1
    width = tokens.shape[1]
    count = 1024
    factor = 1.0 / jnp.sqrt(f32(count))
    grads, all_tokens = gather_tensor(jnp.stack([out_grad, tokens]), core)
    grads = turn(grads, z - x, lo ^ hi).reshape(count, width)
    all_tokens = turn(all_tokens, z - x, lo ^ hi)
    terms = lax.dot_general(down_weight, grads, (((1,), (1,)), ((), ())), preferred_element_type=f32)
    terms = [terms[:, i * 128 : (i + 1) * 128] for i in range(8)]
    first = first_sums(terms)
    pre = gather_dp(jnp.stack([gate_pre.T, up_pre.T]), first)
    own = reduce_dp(terms, first)

    def wgrad(left, right):
        out = lax.dot_general(left, right, (((1,), (0,)), ((), ())), preferred_element_type=f32)
        return (out * factor).astype(bf)

    def back(left, right):
        return lax.dot_general(left, right, (((0,), (0,)), ((), ())), preferred_element_type=f32)

    gate, upper = (jnp.concatenate([p[i] for p in pre], axis=-1) for i in range(2))
    gate, upper = lax.optimization_barrier((gate, upper))
    gate, upper = gate.astype(f32), upper.astype(f32)
    hidden = (gate * jax.nn.sigmoid(gate) * upper).astype(bf)
    down_wgrad = wgrad(hidden, grads)
    sums = ring_gather(own.astype(bf))
    partials, gate_grads, up_grads = [], [], []
    for keys in ORDER:
        gate32 = jnp.concatenate([pre[k][0] for k in keys], axis=-1).astype(f32)
        upper32 = jnp.concatenate([pre[k][1] for k in keys], axis=-1).astype(f32)
        hidden_grad = jnp.concatenate([sums[k] for k in keys], axis=-1)
        if keys == ORDER[1]:
            hidden_grad = after(hidden_grad, down_wgrad)
        hidden_grad = hidden_grad.astype(f32)
        sigma = jax.nn.sigmoid(gate32)
        gate_grad = (hidden_grad * upper32 * sigma * (1.0 + gate32 * (1.0 - sigma))).astype(bf)
        up_grad = (hidden_grad * gate32 * sigma).astype(bf)
        partial = back(gate_grad, gate_weight.T) + back(up_grad, up_weight.T)
        partials += [partial[i * 128 : (i + 1) * 128] for i in range(len(keys))]
        gate_grads.append(gate_grad)
        up_grads.append(up_grad)
    keys = sum(ORDER, ())
    partial = jnp.stack([partials[keys.index(k)] for k in range(8)])
    theirs = lax.dynamic_slice_in_dim(partial, 64 * (1 - core), 64, axis=1)
    mine = lax.dynamic_slice_in_dim(partial, 64 * core, 64, axis=1)
    total = mine + tensor_move(theirs, 0, 0, 1)
    in_grad = sum_chips(turn(total.reshape(4, 2, 64, width), -z, lo).reshape(8, 64, width)).astype(bf)
    held = jnp.concatenate([all_tokens[k // 2, k % 2] for k in keys])
    gate_grads, up_grads = after(gate_grads, total), after(up_grads, total)
    gate_wgrad = wgrad(jnp.concatenate(gate_grads, axis=1), held).T
    up_wgrad = wgrad(jnp.concatenate(up_grads, axis=1), held).T
    return (in_grad, gate_wgrad, up_wgrad, down_wgrad)


def solution(mesh):
    placed = (
        P("tensor", "dp"),
        P("tensor", "dp"),
        P("dp", "tensor"),
        P("dp", "tensor"),
        P("dp", "tensor"),
        P("dp", "tensor"),
        P("tensor", "dp"),
    )
    return jax.shard_map(
        per_device,
        mesh=mesh,
        in_specs=placed,
        out_specs=(P("tensor", "dp"), P("dp", "tensor"), P("dp", "tensor"), P("tensor", "dp")),
        check_vma=False,
    )
```
